32 devices in a mesh: frame: 4 (over y, core), tensor: 8 (over z, x).
Axes of the slice: x: 2, y: 2, z: 4, core: 2. Of those that a mesh axis runs over, the one named last changes fastest.
Arguments:
- latent: bfloat16 [7680, 1152], P('frame', 'tensor'), may hold values from -6 to 6
- timestep: int32 [1], replicated, may hold values from 0 to 999
- frame_pos: int32 [4], P('frame'), may hold values from 0 to 4095
- time_w1: bfloat16 [256, 1152], replicated, may hold values from -0.375 to 0.375
- time_w2: bfloat16 [1152, 1152], P(None, 'tensor'), may hold values from -0.1875 to 0.1875
- ada_w: bfloat16 [1152, 10368], P('tensor'), may hold values from -0.1875 to 0.1875
- w_sqkv: bfloat16 [1152, 3456], P(None, 'tensor'), may hold values from -0.70710678 to 0.70710678
- w_so: bfloat16 [1152, 1152], P('tensor'), may hold values from -0.25 to 0.25
- w_tqkv: bfloat16 [1152, 3456], P(None, 'tensor'), may hold values from -0.70710678 to 0.70710678
- w_to: bfloat16 [1152, 1152], P('tensor'), may hold values from -0.25 to 0.25
- w_fc1: bfloat16 [1152, 4608], P(None, 'tensor'), may hold values from -0.1875 to 0.1875
- w_fc2: bfloat16 [4608, 1152], P('tensor'), may hold values from -0.125 to 0.125
Outputs:
- block_out: bfloat16 [7680, 1152], P('frame', 'tensor')
The draws below stay inside these ranges and needn't reach their ends.
All inputs are finite; a program needn't handle non-finite values.
Results may differ from the reference program's by a relative error of at most 0.025.
Values may be sent and summed in bfloat16 or wider, within the bound.
A program may use at most 128 MiB of HBM per device.

```python
import math
import jax
import jax.numpy as jnp
from jax import lax

D = 1152
H = 16
FF = 4608
TEMB = 256
HD = 72
P_SIZE = 1920
F = 4
TOKENS = 7680
N_TENSOR = 8


def column_gains(key, strong, middle):
    order = jax.random.permutation(key, H)
    gains = jnp.where(order < 2, strong, jnp.where(order < 4, middle, 1.0)).astype(jnp.float32)
    query_or_key = jnp.arange(3 * HD) // HD < 2
    table = jnp.where(query_or_key[None, :], gains[:, None], jnp.float32(1.0))
    return table.reshape(3 * D)


def draw_w_sqkv(key, part):
    key = jax.random.fold_in(key, 11)
    gain_key, value_key = jax.random.split(key)
    base = jax.random.truncated_normal(value_key, -4.0, 4.0, (D, 3 * D), jnp.float32)
    gains = column_gains(gain_key, 5.0, 3.0)
    return (base * gains[None, :] * D ** (-0.5)).astype(jnp.bfloat16)


def draw_w_tqkv(key, part):
    key = jax.random.fold_in(key, 23)
    gain_key, value_key = jax.random.split(key)
    base = jax.random.truncated_normal(value_key, -4.0, 4.0, (D, 3 * D), jnp.float32)
    gains = column_gains(gain_key, 5.0, 3.0)
    return (base * gains[None, :] * D ** (-0.5)).astype(jnp.bfloat16)


def plant(result, stream_key, smallest, high):
    extent = result.shape
    place = [jax.random.randint(jax.random.fold_in(stream_key, axis), (), 0, extent[axis]) for axis in range(len(extent))]
    result = result.at[tuple(place)].set(smallest)
    longest = extent.index(max(extent))
    place[longest] = (place[longest] + 1) % extent[longest]
    return result.at[tuple(place)].set(high)


def with_spikes(values, own_key, source, target, parts, factor):
    owner, partner = [(jnp.arange(values.shape[position]) // (values.shape[position] // parts)).reshape([-1 if axis == position else 1 for axis in range(values.ndim)]) for position in (source, target)]
    chosen = jax.random.permutation(own_key, parts)[partner]
    strong = (owner == chosen) | (owner == (partner + parts // 2) % parts)
    return jnp.where(strong, factor * values, values)


def shard_levels(stream_key, dims, cuts, low, largest):
    def one(position, blocks):
        heights = jax.random.uniform(jax.random.fold_in(jax.random.fold_in(stream_key, 6), position), (blocks,), jnp.float32, low / len(cuts), largest / len(cuts))
        return jnp.repeat(jnp.exp(heights), dims[position] // blocks).reshape((-1,) + (1,) * (len(dims) - position - 1))

    loudness = one(*cuts[0])
    for cut in cuts[1:]:
        loudness = loudness * one(*cut)
    return loudness


def scatter_about(key, extent, scale, limit, shards=(), kind=jnp.bfloat16):
    loudness = shard_levels(key, extent, shards, -0.22, 0.18) if shards else 1.0
    values = jax.random.normal(key, extent, jnp.float32) * scale * loudness
    return jnp.minimum(jnp.maximum(values, -limit), limit).astype(kind)


def heavy_noise(own_key, shape, scale, limit, shards, heavy, held_as=jnp.bfloat16):
    entries = scale * jax.random.normal(own_key, shape, jnp.float32)
    if shards:
        entries = entries * shard_levels(own_key, shape, shards, -0.22, 0.18)
    return jnp.clip(with_spikes(entries, jax.random.fold_in(own_key, 3), *heavy), -limit, limit).astype(held_as)


def setup_inputs(seed: int = 0) -> dict:
    keys = jax.random.split(jax.random.key(seed), 13)
    latent = scatter_about(keys[0], (TOKENS, D), 1.0, 6.0, ((0, 4), (1, 8)))
    timestep = jax.random.randint(keys[1], (1,), 0, 1000).astype(jnp.int32)
    frame_pos = plant(jax.random.randint(keys[2], (F,), 0, 4096), jax.random.fold_in(keys[2], 1), 0, 4095).astype(jnp.int32)
    time_w1 = scatter_about(keys[3], (TEMB, D), TEMB ** -0.5, 0.375)
    time_w2 = scatter_about(keys[4], (D, D), D ** -0.5, 0.1875, ((1, 8),))
    ada_w = scatter_about(keys[5], (D, 9 * D), D ** -0.5, 0.1875, ((0, 8),))
    w_sqkv = draw_w_sqkv(jax.random.fold_in(keys[12], 71), 0)
    w_so = heavy_noise(keys[7], (D, D), D ** -0.5, 0.25, ((0, 8),), (0, 1, 8, 2.0))
    w_tqkv = draw_w_tqkv(jax.random.fold_in(keys[12], 71), 0)
    w_to = heavy_noise(keys[9], (D, D), D ** -0.5, 0.25, ((0, 8),), (0, 1, 8, 2.0))
    w_fc1 = scatter_about(keys[10], (D, FF), D ** -0.5, 0.1875, ((1, 8),))
    w_fc2 = heavy_noise(keys[11], (FF, D), FF ** -0.5, 0.125, ((0, 8),), (0, 1, 8, 2.0))
    return dict(latent=latent, timestep=timestep, frame_pos=frame_pos, time_w1=time_w1, time_w2=time_w2, ada_w=ada_w, w_sqkv=w_sqkv, w_so=w_so, w_tqkv=w_tqkv, w_to=w_to, w_fc1=w_fc1, w_fc2=w_fc2)


def layer_norm(values_in):
    center = values_in - lax.optimization_barrier(jnp.mean(values_in, axis=-1, keepdims=True))
    spread = lax.optimization_barrier(jnp.mean(center * center, axis=-1, keepdims=True))
    return center * lax.rsqrt(spread + 1e-06)

def branch_input(stream, shift, scale):
    return (layer_norm(stream.astype(jnp.float32)) * (1.0 + scale) + shift).astype(jnp.bfloat16)

def time_features(timestep, width):
    half_width = width // 2
    frequency = jnp.exp(-math.log(10000.0) * jnp.arange(half_width, dtype=jnp.float32) / half_width)
    angles = timestep.astype(jnp.float32)[:, None] * frequency[None, :]
    return jnp.concatenate([jnp.cos(angles), jnp.sin(angles)], axis=1).astype(jnp.bfloat16)

def rotate(projected, positions):
    half_width = HD // 2
    frequency = jnp.exp(-math.log(10000.0) * jnp.arange(half_width, dtype=jnp.float32) / half_width)
    angles = positions.astype(jnp.float32)[:, None] * frequency[None, :]
    cosine = jnp.cos(angles)[:, None, None, :]
    sine_part = jnp.sin(angles)[:, None, None, :]

    def turn(section):
        section = section.astype(jnp.float32)
        first_half = section[..., :half_width]
        second_half = section[..., half_width:]
        turned = jnp.concatenate([first_half * cosine - second_half * sine_part, first_half * sine_part + second_half * cosine], axis=-1)
        return turned.astype(jnp.bfloat16)
    return (turn(projected[:, :, :, 0]), turn(projected[:, :, :, 1]), projected[:, :, :, 2])

def grouped(activation, weight):
    group_width = activation.shape[1] // N_TENSOR

    def add_group(index, total):
        start = index * group_width
        columns = lax.dynamic_slice_in_dim(activation, start, group_width, 1)
        rows_part = lax.dynamic_slice_in_dim(weight, start, group_width, 0)
        term = jnp.dot(columns, rows_part, preferred_element_type=jnp.float32).astype(jnp.bfloat16)
        term = lax.optimization_barrier(term)
        return total + term.astype(jnp.float32)
    empty = jnp.zeros((activation.shape[0], weight.shape[1]), jnp.float32)
    return lax.fori_loop(0, N_TENSOR, add_group, empty)

def reference(latent, timestep, frame_pos, time_w1, time_w2, ada_w, w_sqkv, w_so, w_tqkv, w_to, w_fc1, w_fc2):
    time_embed = time_features(timestep, TEMB)
    hidden_time = jax.nn.silu(jnp.dot(time_embed, time_w1, preferred_element_type=jnp.float32)).astype(jnp.bfloat16)
    condition = jax.nn.silu(jnp.dot(hidden_time, time_w2, preferred_element_type=jnp.float32)).astype(jnp.bfloat16)
    modulation = jnp.dot(condition, ada_w, preferred_element_type=jnp.float32)[0]

    def mod_vector(index):
        return modulation[index * D:(index + 1) * D]
    scale_factor = HD ** (-0.5)
    normed = branch_input(latent, mod_vector(0), mod_vector(1))
    projected = jnp.dot(normed, w_sqkv, preferred_element_type=jnp.float32).astype(jnp.bfloat16)
    projected = projected.reshape(F, P_SIZE, H, 3, HD)

    def frame_attention(frame_qkv):
        queries = frame_qkv[:, :, 0].astype(jnp.float32)
        keys_all = frame_qkv[:, :, 1].astype(jnp.float32)
        values_all = frame_qkv[:, :, 2].astype(jnp.float32)
        scores = jnp.einsum('phd,qhd->hpq', queries, keys_all) * scale_factor
        weights = jax.nn.softmax(scores, axis=-1).astype(jnp.bfloat16)
        return jnp.einsum('hpq,qhd->phd', weights.astype(jnp.float32), values_all).astype(jnp.bfloat16)
    attended = lax.map(frame_attention, projected).reshape(TOKENS, D)
    stream = (latent.astype(jnp.float32) + mod_vector(2) * grouped(attended, w_so)).astype(jnp.bfloat16)
    normed = branch_input(stream, mod_vector(3), mod_vector(4))
    projected = jnp.dot(normed, w_tqkv, preferred_element_type=jnp.float32).astype(jnp.bfloat16)
    projected = projected.reshape(F, P_SIZE, H, 3, HD)
    queries, keys_all, values_all = rotate(projected, frame_pos)
    scores = jnp.einsum('fphd,gphd->phfg', queries.astype(jnp.float32), keys_all.astype(jnp.float32)) * scale_factor
    weights = jax.nn.softmax(scores, axis=-1).astype(jnp.bfloat16)
    attended = jnp.einsum('phfg,gphd->fphd', weights.astype(jnp.float32), values_all.astype(jnp.float32)).astype(jnp.bfloat16)
    attended = attended.reshape(TOKENS, D)
    stream = (stream.astype(jnp.float32) + mod_vector(5) * grouped(attended, w_to)).astype(jnp.bfloat16)
    normed = branch_input(stream, mod_vector(6), mod_vector(7))
    mlp_hidden = jax.nn.gelu(jnp.dot(normed, w_fc1, preferred_element_type=jnp.float32), approximate=True).astype(jnp.bfloat16)
    return (stream.astype(jnp.float32) + mod_vector(8) * grouped(mlp_hidden, w_fc2)).astype(jnp.bfloat16)
```

```python
import math

import jax
import jax.numpy as jnp
from jax import lax
from jax.sharding import PartitionSpec as P

D = 1152
HD = 72
P_SIZE = 1920


def layer_norm(values_in):
    center = values_in - jnp.mean(values_in, axis=-1, keepdims=True)
    spread = jnp.mean(center * center, axis=-1, keepdims=True)
    return center * lax.rsqrt(spread + 1e-06)


def branch_input(stream, shift, scale):
    return (layer_norm(stream.astype(jnp.float32)) * (1.0 + scale) + shift).astype(jnp.bfloat16)


def time_features(timestep, width):
    half_width = width // 2
    frequency = jnp.exp(-math.log(10000.0) * jnp.arange(half_width, dtype=jnp.float32) / half_width)
    angles = timestep.astype(jnp.float32)[:, None] * frequency[None, :]
    return jnp.concatenate([jnp.cos(angles), jnp.sin(angles)], axis=1).astype(jnp.bfloat16)


def bdot(a, b):
    return jnp.dot(a, b, preferred_element_type=jnp.float32)


def spatial_attention(normed, w_qkv):
    heads_local = w_qkv.shape[1] // (3 * HD)
    projected = bdot(normed, w_qkv).astype(jnp.bfloat16)
    projected = projected.reshape(P_SIZE, heads_local, 3, HD)
    scores = jnp.einsum(
        "phd,qhd->hpq", projected[:, :, 0], projected[:, :, 1], preferred_element_type=jnp.float32
    ) * HD ** (-0.5)
    weights = jax.nn.softmax(scores, axis=-1).astype(jnp.bfloat16)
    attended = jnp.einsum(
        "hpq,qhd->phd", weights, projected[:, :, 2], preferred_element_type=jnp.float32
    ).astype(jnp.bfloat16)
    return attended.reshape(P_SIZE, heads_local * HD)


def gather_rows(shard, frame_count, frame_index):
    rows = shard.shape[0]
    if rows % frame_count:
        return lax.all_gather(shard, "tensor", axis=0, tiled=True)
    part = rows // frame_count
    mine = lax.dynamic_slice_in_dim(shard, frame_index * part, part, 0)
    return lax.all_gather(mine, ("tensor", "frame"), axis=0, tiled=True)


def gather_columns(shard, frame_count, frame_index):
    part = shard.shape[0] // frame_count
    mine = lax.dynamic_slice_in_dim(shard, frame_index * part, part, 0)
    full = lax.all_gather(mine, ("tensor", "frame"), axis=0, tiled=True)
    return full.reshape(-1, shard.shape[0], shard.shape[1])


def temporal_attention(q, k, v, frame_pos, heads):
    half = HD // 2
    frequency = jnp.exp(-math.log(10000.0) * jnp.arange(half, dtype=jnp.float32) / half)
    angles = frame_pos.astype(jnp.float32)[:, None] * frequency[None, :]
    cosine = jnp.tile(jnp.cos(angles), (1, 2 * heads))[:, None, :]
    sine = jnp.sin(angles)
    sine = jnp.tile(jnp.concatenate([-sine, sine], axis=1), (1, heads))[:, None, :]
    first = (jnp.arange(heads * HD) % HD) < half

    def turn(x):
        x = x.astype(jnp.float32)
        swapped = jnp.where(first, jnp.roll(x, -half, axis=-1), jnp.roll(x, half, axis=-1))
        return (x * cosine + swapped * sine).astype(jnp.bfloat16)

    frames, pp = q.shape[0], q.shape[1]
    q = turn(q).reshape(frames, pp, heads, HD)
    k = turn(k).reshape(frames, pp, heads, HD)
    v = v.reshape(frames, pp, heads, HD)
    scores = jnp.sum(
        q[:, None].astype(jnp.float32) * k[None, :].astype(jnp.float32), axis=-1
    ) * HD ** (-0.5)
    weights = jax.nn.softmax(scores, axis=1).astype(jnp.bfloat16).astype(jnp.float32)
    out = jnp.sum(weights[..., None] * v[None].astype(jnp.float32), axis=1)
    return out.astype(jnp.bfloat16).reshape(frames * pp, heads * HD)


def shards(
    latent, timestep, frame_pos, time_w1, time_w2, ada_w, w_sqkv, w_so, w_tqkv, w_to, w_fc1, w_fc2
):
    frames = lax.axis_size("frame")
    tensors = lax.axis_size("tensor")
    count = frames * tensors
    frame_index = lax.axis_index("frame")
    heads = D // HD
    width = latent.shape[1]
    pp = -(-P_SIZE // (count * 16)) * 16
    padded = count * pp

    time_embed = time_features(timestep, time_w1.shape[0])
    hidden_time = jax.nn.silu(bdot(time_embed, time_w1)).astype(jnp.bfloat16)
    condition = jax.nn.silu(bdot(hidden_time, time_w2)).astype(jnp.bfloat16)
    partial_mod = bdot(condition, ada_w)
    modulation = lax.psum(partial_mod.astype(jnp.bfloat16), "tensor").astype(jnp.float32)[0]

    def mod_vector(index):
        return modulation[index * D : (index + 1) * D]

    def to_patches(block):
        block = jnp.pad(block, ((0, padded - P_SIZE), (0, 0))).reshape(count, pp, width)
        got = lax.all_to_all(block, ("frame", "tensor"), 0, 0, tiled=True)
        got = got.reshape(frames, tensors, pp, width).transpose(0, 2, 1, 3)
        return got.reshape(frames * pp, D)

    def to_features(rows):
        block = rows.reshape(frames, pp, tensors, width).transpose(0, 2, 1, 3)
        got = lax.all_to_all(
            block.reshape(count, pp, width), ("frame", "tensor"), 0, 0, tiled=True
        )
        return got.reshape(padded, width)[:P_SIZE]

    full_rows = lax.all_gather(latent, "tensor", axis=1, tiled=True)
    all_pos = lax.all_gather(frame_pos, "frame", axis=0, tiled=True)
    full_rows, w_so, w_tqkv, w_to, w_fc1, w_fc2 = lax.optimization_barrier(
        (full_rows, w_so, w_tqkv, w_to, w_fc1, w_fc2)
    )
    full_so = gather_rows(w_so, frames, frame_index)
    full_tqkv = gather_columns(w_tqkv, frames, frame_index)
    full_to = gather_rows(w_to, frames, frame_index)
    full_fc1 = gather_columns(w_fc1, frames, frame_index)
    full_fc2 = gather_rows(w_fc2, frames, frame_index)

    residual = to_patches(latent).astype(jnp.float32)
    normed = branch_input(full_rows, mod_vector(0), mod_vector(1))
    attended = to_patches(spatial_attention(normed, w_sqkv))

    stream = (residual + mod_vector(2) * bdot(attended, full_so)).astype(jnp.bfloat16)
    normed = branch_input(stream, mod_vector(3), mod_vector(4))
    qkv = jnp.einsum("rk,tkn->rtn", normed, full_tqkv, preferred_element_type=jnp.float32)
    qkv = qkv.astype(jnp.bfloat16).reshape(frames, pp, heads, 3, HD)
    q, k, v = (qkv[:, :, :, i].reshape(frames, pp, D) for i in range(3))
    attended = temporal_attention(q, k, v, all_pos, heads)
    stream = (stream.astype(jnp.float32) + mod_vector(5) * bdot(attended, full_to)).astype(
        jnp.bfloat16
    )
    normed = branch_input(stream, mod_vector(6), mod_vector(7))
    hidden = jnp.einsum("rk,tkn->rtn", normed, full_fc1, preferred_element_type=jnp.float32)
    hidden = jax.nn.gelu(hidden, approximate=True).astype(jnp.bfloat16)
    hidden = hidden.reshape(frames * pp, -1)
    out = stream.astype(jnp.float32) + mod_vector(8) * bdot(hidden, full_fc2)
    return to_features(out.astype(jnp.bfloat16))


def solution(mesh):
    placed = (
        P("frame", "tensor"),
        P(),
        P("frame"),
        P(),
        P(None, "tensor"),
        P("tensor", None),
        P(None, "tensor"),
        P("tensor", None),
        P(None, "tensor"),
        P("tensor", None),
        P(None, "tensor"),
        P("tensor", None),
    )
    return jax.shard_map(
        shards, mesh=mesh, in_specs=placed, out_specs=P("frame", "tensor"), check_vma=False
    )
```

```python
import math

import jax
import jax.numpy as jnp
from jax import lax
from jax.experimental import pallas as pl
from jax.experimental.pallas import tpu as pltpu
from jax.sharding import PartitionSpec as P

D = 1152
HD = 72
P_SIZE = 1920


def layer_norm(values_in):
    center = values_in - jnp.mean(values_in, axis=-1, keepdims=True)
    spread = jnp.mean(center * center, axis=-1, keepdims=True)
    return center * lax.rsqrt(spread + 1e-06)


def branch_input(stream, shift, scale):
    return (layer_norm(stream.astype(jnp.float32)) * (1.0 + scale) + shift).astype(jnp.bfloat16)


def time_features(timestep, width):
    half_width = width // 2
    frequency = jnp.exp(-math.log(10000.0) * jnp.arange(half_width, dtype=jnp.float32) / half_width)
    angles = timestep.astype(jnp.float32)[:, None] * frequency[None, :]
    return jnp.concatenate([jnp.cos(angles), jnp.sin(angles)], axis=1).astype(jnp.bfloat16)


def bdot(a, b):
    return jnp.dot(a, b, preferred_element_type=jnp.float32)


def ring_place(index, n):
    odd = index % 2
    return (1 - odd) * (index // 2) + odd * (n - 1 - index // 2)


def ring_member(place, n):
    back = place // (n // 2)
    return (1 - back) * (2 * place) + back * (2 * (n - 1 - place) + 1)


def exchange_kernel(n, x_ref, part_ref, full_ref, mods_ref, send, recv, msend, mrecv, local):
    me = lax.axis_index("tensor")
    place = ring_place(me, n)
    rows = x_ref.shape[0]
    half = n // 2
    cut = max(16, -(-rows // 32) * 16)

    def member(offset):
        return ring_member(lax.rem(place + offset + 2 * n, n), n)

    barrier = pltpu.get_barrier_semaphore()
    for k in range(1, n):
        peer = lax.rem(me + k, n)
        pl.semaphore_signal(
            barrier, inc=1, device_id={"tensor": peer}, device_id_type=pl.DeviceIdType.MESH
        )
    pl.semaphore_wait(barrier, n - 1)

    def hop(direction, step, lo, size, owner):
        source = x_ref if step == 0 else full_ref.at[owner]
        return pltpu.make_async_remote_copy(
            src_ref=source.at[pl.ds(lo, size)],
            dst_ref=full_ref.at[owner, pl.ds(lo, size)],
            send_sem=send.at[direction, step],
            recv_sem=recv.at[direction, step],
            device_id={"tensor": member(1 if direction == 0 else -1)},
            device_id_type=pl.DeviceIdType.MESH,
        )

    def span(direction, step):
        if step < half - 1:
            return 0, rows
        return (0, cut) if direction == 0 else (cut, rows - cut)

    def outgoing(direction, step):
        lo, size = span(direction, step)
        return hop(direction, step, lo, size, member(-step if direction == 0 else step))

    def incoming(direction, step):
        lo, size = span(direction, step)
        sign = -1 if direction == 0 else 1
        return hop(direction, step, lo, size, member(sign * (step + 1)))

    def mod_copy(slot, peer):
        return pltpu.make_async_remote_copy(
            src_ref=part_ref,
            dst_ref=mods_ref.at[slot],
            send_sem=msend.at[peer],
            recv_sem=mrecv.at[slot],
            device_id={"tensor": peer},
            device_id_type=pl.DeviceIdType.MESH,
        )

    own = pltpu.make_async_copy(x_ref, full_ref.at[me], local)
    mods_ref[me] = part_ref[...]
    for direction in range(2):
        outgoing(direction, 0).start()
    for k in range(1, n):
        mod_copy(me, lax.rem(me + k, n)).start()
    own.start()
    for step in range(1, half):
        for direction in range(2):
            incoming(direction, step - 1).wait_recv()
            outgoing(direction, step).start()
    for direction in range(2):
        incoming(direction, half - 1).wait_recv()
    for step in range(half):
        for direction in range(2):
            outgoing(direction, step).wait_send()
    for k in range(1, n):
        peer = lax.rem(me + k, n)
        mod_copy(peer, peer).wait_recv()
        mod_copy(me, peer).wait_send()
    own.wait()


def exchange(n, x_block, part):
    half = n // 2
    vmem = pl.BlockSpec(memory_space=pltpu.VMEM)
    return pl.pallas_call(
        lambda *refs: exchange_kernel(n, *refs),
        out_shape=(
            jax.ShapeDtypeStruct((n,) + x_block.shape, x_block.dtype),
            jax.ShapeDtypeStruct((n,) + part.shape, part.dtype),
        ),
        in_specs=[vmem, vmem],
        out_specs=(vmem, vmem),
        scratch_shapes=[
            pltpu.SemaphoreType.DMA((2, half)),
            pltpu.SemaphoreType.DMA((2, half)),
            pltpu.SemaphoreType.DMA((n,)),
            pltpu.SemaphoreType.DMA((n,)),
            pltpu.SemaphoreType.DMA,
        ],
        compiler_params=pltpu.CompilerParams(
            collective_id=0, has_side_effects=True, vmem_limit_bytes=24 * 1024 * 1024
        ),
        cost_estimate=pl.CostEstimate(flops=0, bytes_accessed=100_000_000, transcendentals=0),
        name="exchange",
    )(x_block, part)


def spatial_attention(normed_t, w_qkv):
    heads_local = w_qkv.shape[1] // (3 * HD)
    projected = jnp.einsum(
        "kn,kp->np", w_qkv, normed_t, preferred_element_type=jnp.float32
    ).astype(jnp.bfloat16)
    projected = projected.reshape(heads_local, 3, HD, P_SIZE)
    scores = jnp.einsum(
        "hdp,hdq->hpq", projected[:, 0], projected[:, 1], preferred_element_type=jnp.float32
    ) * HD ** (-0.5)
    weights = jax.nn.softmax(scores, axis=-1).astype(jnp.bfloat16)
    attended = jnp.einsum(
        "hpq,hdq->phd", weights, projected[:, 2], preferred_element_type=jnp.float32
    ).astype(jnp.bfloat16)
    return attended.reshape(P_SIZE, heads_local * HD)


def gather_joined(shard_list, frame_count, frame_index):
    if any(shard.shape[0] % frame_count for shard in shard_list):
        return [lax.all_gather(s, "tensor", axis=0, tiled=True) for s in shard_list]
    mine = []
    for shard in shard_list:
        part = shard.shape[0] // frame_count
        mine.append(lax.dynamic_slice_in_dim(shard, frame_index * part, part, 0))
    full = lax.all_gather(jnp.concatenate(mine, axis=0), ("tensor", "frame"), axis=0)
    out, start = [], 0
    for part in mine:
        out.append(full[:, start : start + part.shape[0]].reshape(-1, part.shape[1]))
        start += part.shape[0]
    return out


def temporal_attention(q, k, v, frame_pos, heads):
    half = HD // 2
    frequency = jnp.exp(-math.log(10000.0) * jnp.arange(half, dtype=jnp.float32) / half)
    angles = frame_pos.astype(jnp.float32)[:, None] * frequency[None, :]
    cosine = jnp.tile(jnp.cos(angles), (1, 2 * heads))[:, None, :]
    sine = jnp.sin(angles)
    sine = jnp.tile(jnp.concatenate([-sine, sine], axis=1), (1, heads))[:, None, :]
    first = (jnp.arange(heads * HD) % HD) < half

    def turn(x):
        x = x.astype(jnp.float32)
        swapped = jnp.where(first, jnp.roll(x, -half, axis=-1), jnp.roll(x, half, axis=-1))
        return (x * cosine + swapped * sine).astype(jnp.bfloat16)

    frames, pp = q.shape[0], q.shape[1]
    q = turn(q).reshape(frames, pp, heads, HD)
    k = turn(k).reshape(frames, pp, heads, HD)
    v = v.reshape(frames, pp, heads, HD)
    scores = jnp.sum(
        q[:, None].astype(jnp.float32) * k[None, :].astype(jnp.float32), axis=-1
    ) * HD ** (-0.5)
    weights = jax.nn.softmax(scores, axis=1).astype(jnp.bfloat16).astype(jnp.float32)
    out = jnp.sum(weights[..., None] * v[None].astype(jnp.float32), axis=1)
    return out.astype(jnp.bfloat16).reshape(frames * pp, heads * HD)


def shards(
    latent, timestep, frame_pos, time_w1, time_w2, ada_w, w_sqkv, w_so, w_tqkv, w_to, w_fc1, w_fc2
):
    frames = lax.axis_size("frame")
    tensors = lax.axis_size("tensor")
    count = frames * tensors
    frame_index = lax.axis_index("frame")
    heads = D // HD
    width = latent.shape[1]
    pp = -(-P_SIZE // (count * 16)) * 16
    padded = count * pp

    time_embed = time_features(timestep, time_w1.shape[0])
    hidden_time = jax.nn.silu(bdot(time_embed, time_w1)).astype(jnp.bfloat16)
    condition = jax.nn.silu(bdot(hidden_time, time_w2)).astype(jnp.bfloat16)
    partial_mod = bdot(condition, ada_w).reshape(-1, 128)
    part_rows = partial_mod.shape[0]
    partial_mod = jnp.pad(partial_mod, ((0, -part_rows % 8), (0, 0)))

    group_one = gather_joined([w_tqkv.T, w_so, w_to], frames, frame_index)
    full_t, mods = exchange(tensors, latent.T, partial_mod)
    full_t = full_t.reshape(D, P_SIZE)
    modulation = jnp.sum(mods, axis=0)[:part_rows].reshape(-1)
    full_t, w_fc1, w_fc2 = lax.optimization_barrier((full_t, w_fc1, w_fc2))
    group_two = gather_joined([w_fc1.T, w_fc2], frames, frame_index)
    full_tqkv, full_so, full_to = group_one
    full_fc1, full_fc2 = group_two

    def mod_vector(index):
        return modulation[index * D : (index + 1) * D]

    def to_patches(block):
        block = jnp.pad(block, ((0, padded - P_SIZE), (0, 0))).reshape(count, pp, width)
        got = lax.all_to_all(block, ("frame", "tensor"), 0, 0, tiled=True)
        got = got.reshape(frames, tensors, pp, width).transpose(0, 2, 1, 3)
        return got.reshape(frames * pp, D)

    def to_features(rows):
        block = rows.reshape(frames, pp, tensors, width).transpose(0, 2, 1, 3)
        got = lax.all_to_all(
            block.reshape(count, pp, width), ("frame", "tensor"), 0, 0, tiled=True
        )
        return got.reshape(padded, width)[:P_SIZE]

    all_pos = lax.all_gather(frame_pos, "frame", axis=0, tiled=True)
    residual = to_patches(latent).astype(jnp.float32)
    rows_t = full_t.astype(jnp.float32)
    center = rows_t - jnp.mean(rows_t, axis=0, keepdims=True)
    spread = jnp.mean(center * center, axis=0, keepdims=True)
    normed_t = center * lax.rsqrt(spread + 1e-06)
    normed_t = normed_t * (1.0 + mod_vector(1))[:, None] + mod_vector(0)[:, None]
    attended = to_patches(spatial_attention(normed_t.astype(jnp.bfloat16), w_sqkv))

    stream = (residual + mod_vector(2) * bdot(attended, full_so)).astype(jnp.bfloat16)
    normed = branch_input(stream, mod_vector(3), mod_vector(4))
    qkv = jnp.einsum("rk,nk->rn", normed, full_tqkv, preferred_element_type=jnp.float32)
    qkv = qkv.astype(jnp.bfloat16).reshape(frames, pp, heads, 3, HD)
    q, k, v = (qkv[:, :, :, i].reshape(frames, pp, D) for i in range(3))
    attended = temporal_attention(q, k, v, all_pos, heads)
    stream = (stream.astype(jnp.float32) + mod_vector(5) * bdot(attended, full_to)).astype(
        jnp.bfloat16
    )
    normed = branch_input(stream, mod_vector(6), mod_vector(7))
    hidden = jnp.einsum("rk,nk->rn", normed, full_fc1, preferred_element_type=jnp.float32)
    hidden = jax.nn.gelu(hidden, approximate=True).astype(jnp.bfloat16)
    out = stream.astype(jnp.float32) + mod_vector(8) * bdot(hidden, full_fc2)
    return to_features(out.astype(jnp.bfloat16))


def solution(mesh):
    placed = (
        P("frame", "tensor"),
        P(),
        P("frame"),
        P(),
        P(None, "tensor"),
        P("tensor", None),
        P(None, "tensor"),
        P("tensor", None),
        P(None, "tensor"),
        P("tensor", None),
        P(None, "tensor"),
        P("tensor", None),
    )
    return jax.shard_map(
        shards, mesh=mesh, in_specs=placed, out_specs=P("frame", "tensor"), check_vma=False
    )
```

```python
import math

import jax
import jax.numpy as jnp
from jax import lax
from jax.experimental import pallas as pl
from jax.experimental.pallas import tpu as pltpu
from jax.sharding import PartitionSpec as P

D = 1152
HD = 72
P_SIZE = 1920


def layer_norm(values_in):
    center = values_in - jnp.mean(values_in, axis=-1, keepdims=True)
    spread = jnp.mean(center * center, axis=-1, keepdims=True)
    return center * lax.rsqrt(spread + 1e-06)


def branch_input(stream, shift, scale):
    return (layer_norm(stream.astype(jnp.float32)) * (1.0 + scale) + shift).astype(jnp.bfloat16)


def time_features(timestep, width):
    half_width = width // 2
    frequency = jnp.exp(-math.log(10000.0) * jnp.arange(half_width, dtype=jnp.float32) / half_width)
    angles = timestep.astype(jnp.float32)[:, None] * frequency[None, :]
    return jnp.concatenate([jnp.cos(angles), jnp.sin(angles)], axis=1).astype(jnp.bfloat16)


def bdot(a, b):
    return jnp.dot(a, b, preferred_element_type=jnp.float32)


def ring_place(index, n):
    odd = index % 2
    return (1 - odd) * (index // 2) + odd * (n - 1 - index // 2)


def ring_member(place, n):
    back = place // (n // 2)
    return (1 - back) * (2 * place) + back * (2 * (n - 1 - place) + 1)


def exchange_kernel(n, x_ref, part_ref, full_ref, mods_ref, send, recv, msend, mrecv, local):
    me = lax.axis_index("tensor")
    place = ring_place(me, n)
    rows = x_ref.shape[0]
    half = n // 2
    cut = max(16, -(-rows // 32) * 16)

    def member(offset):
        return ring_member(lax.rem(place + offset + 2 * n, n), n)

    barrier = pltpu.get_barrier_semaphore()
    for k in range(1, n):
        peer = lax.rem(me + k, n)
        pl.semaphore_signal(
            barrier, inc=1, device_id={"tensor": peer}, device_id_type=pl.DeviceIdType.MESH
        )
    pl.semaphore_wait(barrier, n - 1)

    def hop(direction, step, lo, size, owner):
        source = x_ref if step == 0 else full_ref.at[owner]
        return pltpu.make_async_remote_copy(
            src_ref=source.at[pl.ds(lo, size)],
            dst_ref=full_ref.at[owner, pl.ds(lo, size)],
            send_sem=send.at[direction, step],
            recv_sem=recv.at[direction, step],
            device_id={"tensor": member(1 if direction == 0 else -1)},
            device_id_type=pl.DeviceIdType.MESH,
        )

    def span(direction, step):
        if step < half - 1:
            return 0, rows
        return (0, cut) if direction == 0 else (cut, rows - cut)

    def outgoing(direction, step):
        lo, size = span(direction, step)
        return hop(direction, step, lo, size, member(-step if direction == 0 else step))

    def incoming(direction, step):
        lo, size = span(direction, step)
        sign = -1 if direction == 0 else 1
        return hop(direction, step, lo, size, member(sign * (step + 1)))

    def mod_copy(slot, peer):
        return pltpu.make_async_remote_copy(
            src_ref=part_ref,
            dst_ref=mods_ref.at[slot],
            send_sem=msend.at[peer],
            recv_sem=mrecv.at[slot],
            device_id={"tensor": peer},
            device_id_type=pl.DeviceIdType.MESH,
        )

    own = pltpu.make_async_copy(x_ref, full_ref.at[me], local)
    mods_ref[me] = part_ref[...]
    for direction in range(2):
        outgoing(direction, 0).start()
    for k in range(1, n):
        mod_copy(me, lax.rem(me + k, n)).start()
    own.start()
    for step in range(1, half):
        for direction in range(2):
            incoming(direction, step - 1).wait_recv()
            outgoing(direction, step).start()
    for direction in range(2):
        incoming(direction, half - 1).wait_recv()
    for step in range(half):
        for direction in range(2):
            outgoing(direction, step).wait_send()
    for k in range(1, n):
        peer = lax.rem(me + k, n)
        mod_copy(peer, peer).wait_recv()
        mod_copy(me, peer).wait_send()
    own.wait()


def exchange(n, x_block, part):
    half = n // 2
    vmem = pl.BlockSpec(memory_space=pltpu.VMEM)
    return pl.pallas_call(
        lambda *refs: exchange_kernel(n, *refs),
        out_shape=(
            jax.ShapeDtypeStruct((n,) + x_block.shape, x_block.dtype),
            jax.ShapeDtypeStruct((n,) + part.shape, part.dtype),
        ),
        in_specs=[vmem, vmem],
        out_specs=(vmem, vmem),
        scratch_shapes=[
            pltpu.SemaphoreType.DMA((2, half)),
            pltpu.SemaphoreType.DMA((2, half)),
            pltpu.SemaphoreType.DMA((n,)),
            pltpu.SemaphoreType.DMA((n,)),
            pltpu.SemaphoreType.DMA,
        ],
        compiler_params=pltpu.CompilerParams(
            collective_id=0, has_side_effects=True, vmem_limit_bytes=24 * 1024 * 1024
        ),
        cost_estimate=pl.CostEstimate(flops=0, bytes_accessed=100_000_000, transcendentals=0),
        name="exchange",
    )(x_block, part)


def spatial_attention(normed_t, w_qkv):
    heads_local = w_qkv.shape[1] // (3 * HD)
    projected = jnp.einsum(
        "kn,kp->np", w_qkv, normed_t, preferred_element_type=jnp.float32
    ).astype(jnp.bfloat16)
    projected = projected.reshape(heads_local, 3, HD, P_SIZE)
    scores = jnp.einsum(
        "hdp,hdq->hpq", projected[:, 0], projected[:, 1], preferred_element_type=jnp.float32
    ) * HD ** (-0.5)
    weights = jax.nn.softmax(scores, axis=-1).astype(jnp.bfloat16)
    attended = jnp.einsum(
        "hpq,hdq->phd", weights, projected[:, 2], preferred_element_type=jnp.float32
    ).astype(jnp.bfloat16)
    return attended.reshape(P_SIZE, heads_local * HD)


def gather_joined(shard_list, frame_count, frame_index):
    if any(shard.shape[0] % frame_count for shard in shard_list):
        return [lax.all_gather(s, "tensor", axis=0, tiled=True) for s in shard_list]
    mine = []
    for shard in shard_list:
        part = shard.shape[0] // frame_count
        mine.append(lax.dynamic_slice_in_dim(shard, frame_index * part, part, 0))
    full = lax.all_gather(jnp.concatenate(mine, axis=0), ("tensor", "frame"), axis=0)
    out, start = [], 0
    for part in mine:
        out.append(full[:, start : start + part.shape[0]].reshape(-1, part.shape[1]))
        start += part.shape[0]
    return out


def joined_half(core, first, second):
    half = first.shape[0] // 2
    return jnp.concatenate(
        [lax.dynamic_slice_in_dim(w, core * half, half, 0) for w in (first, second)], axis=0
    )


def ring_blocks(n, block):
    order = [ring_member(place, n) for place in range(n)]
    right = [(order[p], order[(p + 1) % n]) for p in range(n)]
    left = [(b, a) for a, b in right]
    blocks = [block]
    from_left, from_right = block, block
    for step in range(n // 2):
        from_left = lax.ppermute(from_left, "tensor", right)
        blocks.append(from_left)
        if step < n // 2 - 1:
            from_right = lax.ppermute(from_right, "tensor", left)
            blocks.append(from_right)
    return blocks


def temporal_attention(q, k, v, frame_pos, heads):
    half = HD // 2
    frequency = jnp.exp(-math.log(10000.0) * jnp.arange(half, dtype=jnp.float32) / half)
    angles = frame_pos.astype(jnp.float32)[:, None] * frequency[None, :]
    cosine = jnp.tile(jnp.cos(angles), (1, 2 * heads))[:, None, :]
    sine = jnp.sin(angles)
    sine = jnp.tile(jnp.concatenate([-sine, sine], axis=1), (1, heads))[:, None, :]
    first = (jnp.arange(heads * HD) % HD) < half

    def turn(x):
        x = x.astype(jnp.float32)
        swapped = jnp.where(first, jnp.roll(x, -half, axis=-1), jnp.roll(x, half, axis=-1))
        return (x * cosine + swapped * sine).astype(jnp.bfloat16)

    frames, pp = q.shape[0], q.shape[1]
    q = turn(q).reshape(frames, pp, heads, HD)
    k = turn(k).reshape(frames, pp, heads, HD)
    v = v.reshape(frames, pp, heads, HD)
    scores = jnp.sum(
        q[:, None].astype(jnp.float32) * k[None, :].astype(jnp.float32), axis=-1
    ) * HD ** (-0.5)
    weights = jax.nn.softmax(scores, axis=1).astype(jnp.bfloat16).astype(jnp.float32)
    out = jnp.sum(weights[..., None] * v[None].astype(jnp.float32), axis=1)
    return out.astype(jnp.bfloat16).reshape(frames * pp, heads * HD)


def shards(
    latent, timestep, frame_pos, time_w1, time_w2, ada_w, w_sqkv, w_so, w_tqkv, w_to, w_fc1, w_fc2
):
    frames = lax.axis_size("frame")
    tensors = lax.axis_size("tensor")
    count = frames * tensors
    frame_index = lax.axis_index("frame")
    heads = D // HD
    width = latent.shape[1]
    pp = -(-P_SIZE // (count * 16)) * 16
    padded = count * pp

    time_embed = time_features(timestep, time_w1.shape[0])
    hidden_time = jax.nn.silu(bdot(time_embed, time_w1)).astype(jnp.bfloat16)
    condition = jax.nn.silu(bdot(hidden_time, time_w2)).astype(jnp.bfloat16)
    partial_mod = bdot(condition, ada_w).reshape(-1, 128)
    part_rows = partial_mod.shape[0]
    partial_mod = jnp.pad(partial_mod, ((0, -part_rows % 8), (0, 0)))

    full_t, mods = exchange(tensors, latent.T, partial_mod)
    full_t = full_t.reshape(D, P_SIZE)
    modulation = jnp.sum(mods, axis=0)[:part_rows].reshape(-1)
    full_t, w_tqkv, w_so, w_to, w_fc1, w_fc2 = lax.optimization_barrier(
        (full_t, w_tqkv, w_so, w_to, w_fc1, w_fc2)
    )
    full_tqkv, full_so, full_to = gather_joined([w_tqkv.T, w_so, w_to], frames, frame_index)
    mlp_blocks = ring_blocks(tensors, joined_half(frame_index % 2, w_fc1.T, w_fc2))

    def mod_vector(index):
        return modulation[index * D : (index + 1) * D]

    def to_patches(block):
        block = jnp.pad(block, ((0, padded - P_SIZE), (0, 0))).reshape(count, pp, width)
        got = lax.all_to_all(block, ("frame", "tensor"), 0, 0, tiled=True)
        got = got.reshape(frames, tensors, pp, width).transpose(0, 2, 1, 3)
        return got.reshape(frames * pp, D)

    def to_features(rows):
        block = rows.reshape(frames, pp, tensors, width).transpose(0, 2, 1, 3)
        got = lax.all_to_all(
            block.reshape(count, pp, width), ("frame", "tensor"), 0, 0, tiled=True
        )
        return got.reshape(padded, width)[:P_SIZE]

    all_pos = lax.all_gather(frame_pos, "frame", axis=0, tiled=True)
    residual = to_patches(latent).astype(jnp.float32)
    rows_t = full_t.astype(jnp.float32)
    center = rows_t - jnp.mean(rows_t, axis=0, keepdims=True)
    spread = jnp.mean(center * center, axis=0, keepdims=True)
    normed_t = center * lax.rsqrt(spread + 1e-06)
    normed_t = normed_t * (1.0 + mod_vector(1))[:, None] + mod_vector(0)[:, None]
    attended = to_patches(spatial_attention(normed_t.astype(jnp.bfloat16), w_sqkv))

    stream = (residual + mod_vector(2) * bdot(attended, full_so)).astype(jnp.bfloat16)
    normed = branch_input(stream, mod_vector(3), mod_vector(4))
    qkv = jnp.einsum("rk,nk->rn", normed, full_tqkv, preferred_element_type=jnp.float32)
    qkv = qkv.astype(jnp.bfloat16).reshape(frames, pp, heads, 3, HD)
    q, k, v = (qkv[:, :, :, i].reshape(frames, pp, D) for i in range(3))
    attended = temporal_attention(q, k, v, all_pos, heads)
    stream = (stream.astype(jnp.float32) + mod_vector(5) * bdot(attended, full_to)).astype(
        jnp.bfloat16
    )
    normed = branch_input(stream, mod_vector(6), mod_vector(7))
    swap = [(i, i ^ 1) for i in range(frames)]
    both = jnp.concatenate([normed, lax.ppermute(normed, "frame", swap)], axis=0)
    total = jnp.zeros(both.shape, jnp.float32)
    for block in mlp_blocks:
        half = block.shape[0] // 2
        hidden = jnp.einsum("rk,nk->rn", both, block[:half], preferred_element_type=jnp.float32)
        hidden = jax.nn.gelu(hidden, approximate=True).astype(jnp.bfloat16)
        total = total + bdot(hidden, block[half:])
    count_rows = normed.shape[0]
    other = lax.ppermute(total[count_rows:].astype(jnp.bfloat16), "frame", swap)
    summed = total[:count_rows] + other.astype(jnp.float32)
    out = stream.astype(jnp.float32) + mod_vector(8) * summed
    return to_features(out.astype(jnp.bfloat16))


def solution(mesh):
    placed = (
        P("frame", "tensor"),
        P(),
        P("frame"),
        P(),
        P(None, "tensor"),
        P("tensor", None),
        P(None, "tensor"),
        P("tensor", None),
        P(None, "tensor"),
        P("tensor", None),
        P(None, "tensor"),
        P("tensor", None),
    )
    return jax.shard_map(
        shards, mesh=mesh, in_specs=placed, out_specs=P("frame", "tensor"), check_vma=False
    )
```

```python
import math

import jax
import jax.numpy as jnp
from jax import lax
from jax.experimental import pallas as pl
from jax.experimental.pallas import tpu as pltpu
from jax.sharding import PartitionSpec as P

D = 1152
HD = 72
P_SIZE = 1920


def layer_norm(values_in):
    center = values_in - jnp.mean(values_in, axis=-1, keepdims=True)
    spread = jnp.mean(center * center, axis=-1, keepdims=True)
    return center * lax.rsqrt(spread + 1e-06)


def branch_input(stream, shift, scale):
    return (layer_norm(stream.astype(jnp.float32)) * (1.0 + scale) + shift).astype(jnp.bfloat16)


def time_features(timestep, width):
    half_width = width // 2
    frequency = jnp.exp(-math.log(10000.0) * jnp.arange(half_width, dtype=jnp.float32) / half_width)
    angles = timestep.astype(jnp.float32)[:, None] * frequency[None, :]
    return jnp.concatenate([jnp.cos(angles), jnp.sin(angles)], axis=1).astype(jnp.bfloat16)


def bdot(a, b):
    return jnp.dot(a, b, preferred_element_type=jnp.float32)


def ring_place(index, n):
    odd = index % 2
    return (1 - odd) * (index // 2) + odd * (n - 1 - index // 2)


def ring_member(place, n):
    back = place // (n // 2)
    return (1 - back) * (2 * place) + back * (2 * (n - 1 - place) + 1)


def exchange_kernel(n, x_ref, part_ref, full_ref, mods_ref, send, recv, msend, mrecv, local):
    me = lax.axis_index("tensor")
    place = ring_place(me, n)
    rows = x_ref.shape[0]
    half = n // 2
    cut = max(16, -(-rows // 32) * 16)

    def member(offset):
        return ring_member(lax.rem(place + offset + 2 * n, n), n)

    barrier = pltpu.get_barrier_semaphore()
    for k in range(1, n):
        peer = lax.rem(me + k, n)
        pl.semaphore_signal(
            barrier, inc=1, device_id={"tensor": peer}, device_id_type=pl.DeviceIdType.MESH
        )
    pl.semaphore_wait(barrier, n - 1)

    def hop(direction, step, lo, size, owner):
        source = x_ref if step == 0 else full_ref.at[owner]
        return pltpu.make_async_remote_copy(
            src_ref=source.at[pl.ds(lo, size)],
            dst_ref=full_ref.at[owner, pl.ds(lo, size)],
            send_sem=send.at[direction, step],
            recv_sem=recv.at[direction, step],
            device_id={"tensor": member(1 if direction == 0 else -1)},
            device_id_type=pl.DeviceIdType.MESH,
        )

    def span(direction, step):
        if step < half - 1:
            return 0, rows
        return (0, cut) if direction == 0 else (cut, rows - cut)

    def outgoing(direction, step):
        lo, size = span(direction, step)
        return hop(direction, step, lo, size, member(-step if direction == 0 else step))

    def incoming(direction, step):
        lo, size = span(direction, step)
        sign = -1 if direction == 0 else 1
        return hop(direction, step, lo, size, member(sign * (step + 1)))

    def mod_copy(slot, peer):
        return pltpu.make_async_remote_copy(
            src_ref=part_ref,
            dst_ref=mods_ref.at[slot],
            send_sem=msend.at[peer],
            recv_sem=mrecv.at[slot],
            device_id={"tensor": peer},
            device_id_type=pl.DeviceIdType.MESH,
        )

    own = pltpu.make_async_copy(x_ref, full_ref.at[me], local)
    mods_ref[me] = part_ref[...]
    for direction in range(2):
        outgoing(direction, 0).start()
    for k in range(1, n):
        mod_copy(me, lax.rem(me + k, n)).start()
    own.start()
    for step in range(1, half):
        for direction in range(2):
            incoming(direction, step - 1).wait_recv()
            outgoing(direction, step).start()
    for direction in range(2):
        incoming(direction, half - 1).wait_recv()
    for step in range(half):
        for direction in range(2):
            outgoing(direction, step).wait_send()
    for k in range(1, n):
        peer = lax.rem(me + k, n)
        mod_copy(peer, peer).wait_recv()
        mod_copy(me, peer).wait_send()
    own.wait()


def exchange(n, x_block, part):
    half = n // 2
    vmem = pl.BlockSpec(memory_space=pltpu.VMEM)
    return pl.pallas_call(
        lambda *refs: exchange_kernel(n, *refs),
        out_shape=(
            jax.ShapeDtypeStruct((n,) + x_block.shape, x_block.dtype),
            jax.ShapeDtypeStruct((n,) + part.shape, part.dtype),
        ),
        in_specs=[vmem, vmem],
        out_specs=(vmem, vmem),
        scratch_shapes=[
            pltpu.SemaphoreType.DMA((2, half)),
            pltpu.SemaphoreType.DMA((2, half)),
            pltpu.SemaphoreType.DMA((n,)),
            pltpu.SemaphoreType.DMA((n,)),
            pltpu.SemaphoreType.DMA,
        ],
        compiler_params=pltpu.CompilerParams(
            collective_id=0, has_side_effects=True, vmem_limit_bytes=24 * 1024 * 1024
        ),
        cost_estimate=pl.CostEstimate(flops=0, bytes_accessed=100_000_000, transcendentals=0),
        name="exchange",
    )(x_block, part)


def spatial_attention(normed_t, w_qkv):
    heads_local = w_qkv.shape[1] // (3 * HD)
    projected = jnp.einsum(
        "kn,kp->np", w_qkv, normed_t, preferred_element_type=jnp.float32
    ).astype(jnp.bfloat16)
    projected = projected.reshape(heads_local, 3, HD, P_SIZE)
    scores = jnp.einsum(
        "hdp,hdq->hpq", projected[:, 0], projected[:, 1], preferred_element_type=jnp.float32
    ) * HD ** (-0.5)
    weights = jax.nn.softmax(scores, axis=-1).astype(jnp.bfloat16)
    attended = jnp.einsum(
        "hpq,hdq->phd", weights, projected[:, 2], preferred_element_type=jnp.float32
    ).astype(jnp.bfloat16)
    return attended.reshape(P_SIZE, heads_local * HD)


HALF = HD // 2
SLOT = -(-HALF // 16) * 16


def padded_halves(rows):
    split = rows.reshape((-1, HALF) + rows.shape[1:])
    return jnp.pad(split, ((0, 0), (0, SLOT - HALF)) + ((0, 0),) * (rows.ndim - 1))


def gather_units(units, frame_count, frame_index):
    if units.shape[0] % frame_count:
        full = lax.all_gather(units, "tensor", axis=0, tiled=True)
        return full
    part = units.shape[0] // frame_count
    mine = lax.dynamic_slice_in_dim(units, frame_index * part, part, 0)
    return lax.all_gather(mine, ("tensor", "frame"), axis=0, tiled=True)


def joined_half(core, first, second):
    half = first.shape[0] // 2
    return jnp.concatenate(
        [lax.dynamic_slice_in_dim(w, core * half, half, 0) for w in (first, second)], axis=0
    )


def ring_blocks(n, block):
    order = [ring_member(place, n) for place in range(n)]
    right = [(order[p], order[(p + 1) % n]) for p in range(n)]
    left = [(b, a) for a, b in right]
    blocks = [block]
    from_left, from_right = block, block
    for step in range(n // 2):
        from_left = lax.ppermute(from_left, "tensor", right)
        blocks.append(from_left)
        if step < n // 2 - 1:
            from_right = lax.ppermute(from_right, "tensor", left)
            blocks.append(from_right)
    return blocks


def temporal_kernel(frames, q_ref, k_ref, v_ref, cos_ref, sin_ref, o_ref):
    rows, width = q_ref.shape
    pp = rows // frames
    lane = lax.broadcasted_iota(jnp.int32, (pp, width), 1)
    first = lane % (2 * SLOT) < SLOT
    gather = (
        lax.broadcasted_iota(jnp.int32, (width, 128), 0) // (2 * SLOT)
        == lax.broadcasted_iota(jnp.int32, (width, 128), 1)
    ).astype(jnp.bfloat16)
    spread = (
        lax.broadcasted_iota(jnp.int32, (128, width), 1) // (2 * SLOT)
        == lax.broadcasted_iota(jnp.int32, (128, width), 0)
    ).astype(jnp.bfloat16)

    def turned(ref, f):
        x = ref[f * pp : (f + 1) * pp, :].astype(jnp.float32)
        partner = jnp.where(
            first, pltpu.roll(x, width - SLOT, axis=1), pltpu.roll(x, SLOT, axis=1)
        )
        x = x * cos_ref[f : f + 1, :] + partner * sin_ref[f : f + 1, :]
        return x.astype(jnp.bfloat16).astype(jnp.float32)

    keys = [turned(k_ref, f) for f in range(frames)]
    for f in range(frames):
        query = turned(q_ref, f)
        product = jnp.concatenate([query * key for key in keys], axis=0)
        high = product.astype(jnp.bfloat16)
        low = (product - high.astype(jnp.float32)).astype(jnp.bfloat16)
        scores = (bdot(high, gather) + bdot(low, gather)) * HD ** (-0.5)
        parts = [scores[g * pp : (g + 1) * pp] for g in range(frames)]
        top = parts[0]
        for part in parts[1:]:
            top = jnp.maximum(top, part)
        parts = [jnp.exp(part - top) for part in parts]
        total = parts[0]
        for part in parts[1:]:
            total = total + part
        weights = [(part / total).astype(jnp.bfloat16) for part in parts]
        wide = bdot(jnp.concatenate(weights, axis=0), spread)
        out = jnp.zeros((pp, width), jnp.float32)
        for g in range(frames):
            rows_g = slice(g * pp, (g + 1) * pp)
            out = out + wide[rows_g] * v_ref[rows_g, :].astype(jnp.float32)
        o_ref[f * pp : (f + 1) * pp, :] = out.astype(jnp.bfloat16)


def temporal_attention(q, k, v, frame_pos):
    frames = frame_pos.shape[0]
    frequency = jnp.exp(-math.log(10000.0) * jnp.arange(HALF, dtype=jnp.float32) / HALF)
    angles = frame_pos.astype(jnp.float32)[:, None] * frequency[None, :]
    fill = ((0, 0), (0, SLOT - HALF))
    cosine = jnp.pad(jnp.cos(angles), fill)
    sine = jnp.pad(jnp.sin(angles), fill)
    slots = q.shape[1] // SLOT
    cosine = jnp.tile(cosine, (1, slots))
    sine = jnp.tile(jnp.concatenate([-sine, sine], axis=1), (1, slots // 2))
    vmem = pl.BlockSpec(memory_space=pltpu.VMEM)
    return pl.pallas_call(
        lambda *refs: temporal_kernel(frames, *refs),
        out_shape=jax.ShapeDtypeStruct(q.shape, q.dtype),
        in_specs=[vmem] * 5,
        out_specs=vmem,
        compiler_params=pltpu.CompilerParams(vmem_limit_bytes=32 * 1024 * 1024),
        name="temporal",
    )(q, k, v, cosine, sine)


def shards(
    latent, timestep, frame_pos, time_w1, time_w2, ada_w, w_sqkv, w_so, w_tqkv, w_to, w_fc1, w_fc2
):
    frames = lax.axis_size("frame")
    tensors = lax.axis_size("tensor")
    count = frames * tensors
    frame_index = lax.axis_index("frame")
    width = latent.shape[1]
    pp = -(-P_SIZE // (count * 16)) * 16
    padded = count * pp

    time_embed = time_features(timestep, time_w1.shape[0])
    hidden_time = jax.nn.silu(bdot(time_embed, time_w1)).astype(jnp.bfloat16)
    condition = jax.nn.silu(bdot(hidden_time, time_w2)).astype(jnp.bfloat16)
    partial_mod = bdot(condition, ada_w).reshape(-1, 128)
    part_rows = partial_mod.shape[0]
    partial_mod = jnp.pad(partial_mod, ((0, -part_rows % 8), (0, 0)))

    qkv_units = w_tqkv.T.reshape(-1, 3, 2, HALF, D).transpose(0, 2, 1, 3, 4)
    qkv_units = jnp.pad(qkv_units, ((0, 0),) * 3 + ((0, SLOT - HALF), (0, 0)))
    units = jnp.concatenate(
        [qkv_units.reshape(-1, 3 * SLOT, D), padded_halves(w_so), padded_halves(w_to)], axis=1
    )
    gathered = gather_units(units, frames, frame_index)
    wq, wk, wv, full_so, full_to = (
        gathered[:, i * SLOT : (i + 1) * SLOT].reshape(-1, D) for i in range(5)
    )
    all_pos = lax.all_gather(frame_pos, "frame", axis=0, tiled=True)

    full_t, mods = exchange(tensors, latent.T, partial_mod)
    full_t = full_t.reshape(D, P_SIZE)
    modulation = jnp.sum(mods, axis=0)[:part_rows].reshape(-1)
    full_t, w_fc1, w_fc2 = lax.optimization_barrier((full_t, w_fc1, w_fc2))
    mlp_blocks = ring_blocks(tensors, joined_half(frame_index % 2, w_fc1.T, w_fc2))

    def mod_vector(index):
        return modulation[index * D : (index + 1) * D]

    def to_patches(block):
        own = block.shape[1]
        block = jnp.pad(block, ((0, padded - P_SIZE), (0, 0))).reshape(count, pp, own)
        got = lax.all_to_all(block, ("frame", "tensor"), 0, 0, tiled=True)
        return got.reshape(frames, tensors, pp, own).transpose(0, 2, 1, 3)

    def to_features(rows):
        block = rows.reshape(frames, pp, tensors, width).transpose(0, 2, 1, 3)
        got = lax.all_to_all(
            block.reshape(count, pp, width), ("frame", "tensor"), 0, 0, tiled=True
        )
        return got.reshape(padded, width)[:P_SIZE]

    rows_t = full_t.astype(jnp.float32)
    center = rows_t - jnp.mean(rows_t, axis=0, keepdims=True)
    spread = jnp.mean(center * center, axis=0, keepdims=True)
    normed_t = center * lax.rsqrt(spread + 1e-06)
    normed_t = normed_t * (1.0 + mod_vector(1))[:, None] + mod_vector(0)[:, None]
    attended = spatial_attention(normed_t.astype(jnp.bfloat16), w_sqkv)
    attended = jnp.pad(
        attended.reshape(P_SIZE, -1, HALF), ((0, 0), (0, 0), (0, SLOT - HALF))
    ).reshape(P_SIZE, -1)
    slot_width = attended.shape[1]
    arrived = to_patches(jnp.concatenate([attended, latent], axis=1))
    attended = arrived[..., :slot_width].reshape(frames * pp, -1)
    residual = arrived[..., slot_width:].reshape(frames * pp, D).astype(jnp.float32)

    def rows_by(a, w):
        return jnp.einsum("rk,nk->rn", a, w, preferred_element_type=jnp.float32)

    stream = (residual + mod_vector(2) * bdot(attended, full_so)).astype(jnp.bfloat16)
    normed = branch_input(stream, mod_vector(3), mod_vector(4))
    q, k, v = (rows_by(normed, w).astype(jnp.bfloat16) for w in (wq, wk, wv))
    attended = temporal_attention(q, k, v, all_pos)
    stream = (stream.astype(jnp.float32) + mod_vector(5) * bdot(attended, full_to)).astype(
        jnp.bfloat16
    )
    normed = branch_input(stream, mod_vector(6), mod_vector(7))
    swap = [(i, i ^ 1) for i in range(frames)]
    both = jnp.concatenate([normed, lax.ppermute(normed, "frame", swap)], axis=0)
    half = mlp_blocks[0].shape[0] // 2
    first = jnp.concatenate([block[:half] for block in mlp_blocks], axis=0)
    second = jnp.concatenate([block[half:] for block in mlp_blocks], axis=0)
    hidden = jax.nn.gelu(rows_by(both, first), approximate=True).astype(jnp.bfloat16)
    total = bdot(hidden, second)
    count_rows = normed.shape[0]
    other = lax.ppermute(total[count_rows:].astype(jnp.bfloat16), "frame", swap)
    summed = total[:count_rows] + other.astype(jnp.float32)
    out = stream.astype(jnp.float32) + mod_vector(8) * summed
    return to_features(out.astype(jnp.bfloat16))


def solution(mesh):
    placed = (
        P("frame", "tensor"),
        P(),
        P("frame"),
        P(),
        P(None, "tensor"),
        P("tensor", None),
        P(None, "tensor"),
        P("tensor", None),
        P(None, "tensor"),
        P("tensor", None),
        P(None, "tensor"),
        P("tensor", None),
    )
    return jax.shard_map(
        shards, mesh=mesh, in_specs=placed, out_specs=P("frame", "tensor"), check_vma=False
    )
```

```python
import math

import jax
import jax.numpy as jnp
from jax import lax
from jax.experimental import pallas as pl
from jax.experimental.pallas import tpu as pltpu
from jax.sharding import PartitionSpec as P

D = 1152
HD = 72
P_SIZE = 1920


def layer_norm(values_in):
    center = values_in - jnp.mean(values_in, axis=-1, keepdims=True)
    spread = jnp.mean(center * center, axis=-1, keepdims=True)
    return center * lax.rsqrt(spread + 1e-06)


def branch_input(stream, shift, scale):
    return (layer_norm(stream.astype(jnp.float32)) * (1.0 + scale) + shift).astype(jnp.bfloat16)


def time_features(timestep, width):
    half_width = width // 2
    frequency = jnp.exp(-math.log(10000.0) * jnp.arange(half_width, dtype=jnp.float32) / half_width)
    angles = timestep.astype(jnp.float32)[:, None] * frequency[None, :]
    return jnp.concatenate([jnp.cos(angles), jnp.sin(angles)], axis=1).astype(jnp.bfloat16)


def bdot(a, b):
    return jnp.dot(a, b, preferred_element_type=jnp.float32)


def ring_place(index, n):
    odd = index % 2
    return (1 - odd) * (index // 2) + odd * (n - 1 - index // 2)


def ring_member(place, n):
    back = place // (n // 2)
    return (1 - back) * (2 * place) + back * (2 * (n - 1 - place) + 1)


def exchange_kernel(n, x_ref, part_ref, full_ref, mods_ref, send, recv, msend, mrecv, local):
    me = lax.axis_index("tensor")
    place = ring_place(me, n)
    rows = x_ref.shape[0]
    half = n // 2
    cut = max(16, -(-rows // 32) * 16)

    def member(offset):
        return ring_member(lax.rem(place + offset + 2 * n, n), n)

    barrier = pltpu.get_barrier_semaphore()
    for k in range(1, n):
        peer = lax.rem(me + k, n)
        pl.semaphore_signal(
            barrier, inc=1, device_id={"tensor": peer}, device_id_type=pl.DeviceIdType.MESH
        )
    pl.semaphore_wait(barrier, n - 1)

    def hop(direction, step, lo, size, owner):
        source = x_ref if step == 0 else full_ref.at[owner]
        return pltpu.make_async_remote_copy(
            src_ref=source.at[pl.ds(lo, size)],
            dst_ref=full_ref.at[owner, pl.ds(lo, size)],
            send_sem=send.at[direction, step],
            recv_sem=recv.at[direction, step],
            device_id={"tensor": member(1 if direction == 0 else -1)},
            device_id_type=pl.DeviceIdType.MESH,
        )

    def span(direction, step):
        if step < half - 1:
            return 0, rows
        return (0, cut) if direction == 0 else (cut, rows - cut)

    def outgoing(direction, step):
        lo, size = span(direction, step)
        return hop(direction, step, lo, size, member(-step if direction == 0 else step))

    def incoming(direction, step):
        lo, size = span(direction, step)
        sign = -1 if direction == 0 else 1
        return hop(direction, step, lo, size, member(sign * (step + 1)))

    def mod_copy(slot, peer):
        return pltpu.make_async_remote_copy(
            src_ref=part_ref,
            dst_ref=mods_ref.at[slot],
            send_sem=msend.at[peer],
            recv_sem=mrecv.at[slot],
            device_id={"tensor": peer},
            device_id_type=pl.DeviceIdType.MESH,
        )

    own = pltpu.make_async_copy(x_ref, full_ref.at[me], local)
    mods_ref[me] = part_ref[...]
    for direction in range(2):
        outgoing(direction, 0).start()
    for k in range(1, n):
        mod_copy(me, lax.rem(me + k, n)).start()
    own.start()
    for step in range(1, half):
        for direction in range(2):
            incoming(direction, step - 1).wait_recv()
            outgoing(direction, step).start()
    for direction in range(2):
        incoming(direction, half - 1).wait_recv()
    for step in range(half):
        for direction in range(2):
            outgoing(direction, step).wait_send()
    for k in range(1, n):
        peer = lax.rem(me + k, n)
        mod_copy(peer, peer).wait_recv()
        mod_copy(me, peer).wait_send()
    own.wait()


def exchange(n, x_block, part):
    half = n // 2
    vmem = pl.BlockSpec(memory_space=pltpu.VMEM)
    return pl.pallas_call(
        lambda *refs: exchange_kernel(n, *refs),
        out_shape=(
            jax.ShapeDtypeStruct((n,) + x_block.shape, x_block.dtype),
            jax.ShapeDtypeStruct((n,) + part.shape, part.dtype),
        ),
        in_specs=[vmem, vmem],
        out_specs=(vmem, vmem),
        scratch_shapes=[
            pltpu.SemaphoreType.DMA((2, half)),
            pltpu.SemaphoreType.DMA((2, half)),
            pltpu.SemaphoreType.DMA((n,)),
            pltpu.SemaphoreType.DMA((n,)),
            pltpu.SemaphoreType.DMA,
        ],
        compiler_params=pltpu.CompilerParams(
            collective_id=0, has_side_effects=True, vmem_limit_bytes=24 * 1024 * 1024
        ),
        cost_estimate=pl.CostEstimate(flops=0, bytes_accessed=100_000_000, transcendentals=0),
        name="exchange",
    )(x_block, part)


def spatial_attention(normed_t, w_qkv):
    heads_local = w_qkv.shape[1] // (3 * HD)
    projected = jnp.einsum(
        "kn,kp->np", w_qkv, normed_t, preferred_element_type=jnp.float32
    ).astype(jnp.bfloat16)
    projected = projected.reshape(heads_local, 3, HD, P_SIZE)
    scores = jnp.einsum(
        "hdp,hdq->hpq", projected[:, 0], projected[:, 1], preferred_element_type=jnp.float32
    ) * HD ** (-0.5)
    weights = jax.nn.softmax(scores, axis=-1).astype(jnp.bfloat16)
    attended = jnp.einsum(
        "hpq,hdq->phd", weights, projected[:, 2], preferred_element_type=jnp.float32
    ).astype(jnp.bfloat16)
    return attended.reshape(P_SIZE, heads_local * HD)


HALF = HD // 2
SLOT = -(-HALF // 16) * 16


def padded_halves(rows):
    split = rows.reshape((-1, HALF) + rows.shape[1:])
    return jnp.pad(split, ((0, 0), (0, SLOT - HALF)) + ((0, 0),) * (rows.ndim - 1))


def gather_units(units, frame_count, frame_index):
    if units.shape[0] % frame_count:
        full = lax.all_gather(units, "tensor", axis=0, tiled=True)
        return full
    part = units.shape[0] // frame_count
    mine = lax.dynamic_slice_in_dim(units, frame_index * part, part, 0)
    return lax.all_gather(mine, ("tensor", "frame"), axis=0, tiled=True)


def joined_half(core, first, second):
    half = first.shape[0] // 2
    return jnp.concatenate(
        [lax.dynamic_slice_in_dim(w, core * half, half, 0) for w in (first, second)], axis=0
    )


def ring_blocks(n, block):
    order = [ring_member(place, n) for place in range(n)]
    right = [(order[p], order[(p + 1) % n]) for p in range(n)]
    left = [(b, a) for a, b in right]
    blocks = [block]
    from_left, from_right = block, block
    for _ in range(n // 2 - 1):
        from_left = lax.ppermute(from_left, "tensor", right)
        from_right = lax.ppermute(from_right, "tensor", left)
        blocks += [from_left, from_right]
    half = block.shape[0] // 2
    upper = lax.ppermute(from_left[:half], "tensor", right)
    lower = lax.ppermute(from_right[half:], "tensor", left)
    blocks.append(jnp.concatenate([upper, lower], axis=0))
    return blocks


def temporal_kernel(frames, q_ref, k_ref, v_ref, cos_ref, sin_ref, o_ref):
    rows, width = q_ref.shape
    pp = rows // frames
    lane = lax.broadcasted_iota(jnp.int32, (pp, width), 1)
    first = lane % (2 * SLOT) < SLOT
    gather = (
        lax.broadcasted_iota(jnp.int32, (width, 128), 0) // (2 * SLOT)
        == lax.broadcasted_iota(jnp.int32, (width, 128), 1)
    ).astype(jnp.bfloat16)
    spread = (
        lax.broadcasted_iota(jnp.int32, (128, width), 1) // (2 * SLOT)
        == lax.broadcasted_iota(jnp.int32, (128, width), 0)
    ).astype(jnp.bfloat16)

    def turned(ref, f):
        x = ref[f * pp : (f + 1) * pp, :].astype(jnp.float32)
        partner = jnp.where(
            first, pltpu.roll(x, width - SLOT, axis=1), pltpu.roll(x, SLOT, axis=1)
        )
        x = x * cos_ref[f : f + 1, :] + partner * sin_ref[f : f + 1, :]
        return x.astype(jnp.bfloat16).astype(jnp.float32)

    keys = [turned(k_ref, f) for f in range(frames)]
    for f in range(frames):
        query = turned(q_ref, f)
        product = jnp.concatenate([query * key for key in keys], axis=0)
        high = product.astype(jnp.bfloat16)
        low = (product - high.astype(jnp.float32)).astype(jnp.bfloat16)
        scores = (bdot(high, gather) + bdot(low, gather)) * HD ** (-0.5)
        parts = [scores[g * pp : (g + 1) * pp] for g in range(frames)]
        top = parts[0]
        for part in parts[1:]:
            top = jnp.maximum(top, part)
        parts = [jnp.exp(part - top) for part in parts]
        total = parts[0]
        for part in parts[1:]:
            total = total + part
        weights = [(part / total).astype(jnp.bfloat16) for part in parts]
        wide = bdot(jnp.concatenate(weights, axis=0), spread)
        out = jnp.zeros((pp, width), jnp.float32)
        for g in range(frames):
            rows_g = slice(g * pp, (g + 1) * pp)
            out = out + wide[rows_g] * v_ref[rows_g, :].astype(jnp.float32)
        o_ref[f * pp : (f + 1) * pp, :] = out.astype(jnp.bfloat16)


def temporal_attention(q, k, v, frame_pos):
    frames = frame_pos.shape[0]
    frequency = jnp.exp(-math.log(10000.0) * jnp.arange(HALF, dtype=jnp.float32) / HALF)
    angles = frame_pos.astype(jnp.float32)[:, None] * frequency[None, :]
    fill = ((0, 0), (0, SLOT - HALF))
    cosine = jnp.pad(jnp.cos(angles), fill)
    sine = jnp.pad(jnp.sin(angles), fill)
    slots = q.shape[1] // SLOT
    cosine = jnp.tile(cosine, (1, slots))
    sine = jnp.tile(jnp.concatenate([-sine, sine], axis=1), (1, slots // 2))
    vmem = pl.BlockSpec(memory_space=pltpu.VMEM)
    return pl.pallas_call(
        lambda *refs: temporal_kernel(frames, *refs),
        out_shape=jax.ShapeDtypeStruct(q.shape, q.dtype),
        in_specs=[vmem] * 5,
        out_specs=vmem,
        compiler_params=pltpu.CompilerParams(vmem_limit_bytes=32 * 1024 * 1024),
        name="temporal",
    )(q, k, v, cosine, sine)


def shards(
    latent, timestep, frame_pos, time_w1, time_w2, ada_w, w_sqkv, w_so, w_tqkv, w_to, w_fc1, w_fc2
):
    frames = lax.axis_size("frame")
    tensors = lax.axis_size("tensor")
    count = frames * tensors
    frame_index = lax.axis_index("frame")
    width = latent.shape[1]
    pp = -(-P_SIZE // (count * 16)) * 16
    padded = count * pp

    time_embed = time_features(timestep, time_w1.shape[0])
    hidden_time = jax.nn.silu(bdot(time_embed, time_w1)).astype(jnp.bfloat16)
    condition = jax.nn.silu(bdot(hidden_time, time_w2)).astype(jnp.bfloat16)
    partial_mod = bdot(condition, ada_w).reshape(-1, 128)
    part_rows = partial_mod.shape[0]
    partial_mod = jnp.pad(partial_mod, ((0, -part_rows % 8), (0, 0)))

    qkv_units = w_tqkv.T.reshape(-1, 3, 2, HALF, D).transpose(0, 2, 1, 3, 4)
    qkv_units = jnp.pad(qkv_units, ((0, 0),) * 3 + ((0, SLOT - HALF), (0, 0)))
    units = jnp.concatenate(
        [qkv_units.reshape(-1, 3 * SLOT, D), padded_halves(w_so), padded_halves(w_to)], axis=1
    )
    gathered = gather_units(units, frames, frame_index)
    wq, wk, wv, full_so, full_to = (
        gathered[:, i * SLOT : (i + 1) * SLOT].reshape(-1, D) for i in range(5)
    )
    all_pos = lax.all_gather(frame_pos, "frame", axis=0, tiled=True)

    full_t, mods = exchange(tensors, latent.T, partial_mod)
    full_t = full_t.reshape(D, P_SIZE)
    modulation = jnp.sum(mods, axis=0)[:part_rows].reshape(-1)
    full_t, w_fc1, w_fc2 = lax.optimization_barrier((full_t, w_fc1, w_fc2))
    mlp_blocks = ring_blocks(tensors, joined_half(frame_index % 2, w_fc1.T, w_fc2))

    def mod_vector(index):
        return modulation[index * D : (index + 1) * D]

    def to_patches(block):
        own = block.shape[1]
        block = jnp.pad(block, ((0, padded - P_SIZE), (0, 0))).reshape(count, pp, own)
        got = lax.all_to_all(block, ("frame", "tensor"), 0, 0, tiled=True)
        return got.reshape(frames, tensors, pp, own).transpose(0, 2, 1, 3)

    def to_features(rows):
        block = rows.reshape(frames, pp, tensors, width).transpose(0, 2, 1, 3)
        got = lax.all_to_all(
            block.reshape(count, pp, width), ("frame", "tensor"), 0, 0, tiled=True
        )
        return got.reshape(padded, width)[:P_SIZE]

    rows_t = full_t.astype(jnp.float32)
    center = rows_t - jnp.mean(rows_t, axis=0, keepdims=True)
    spread = jnp.mean(center * center, axis=0, keepdims=True)
    normed_t = center * lax.rsqrt(spread + 1e-06)
    normed_t = normed_t * (1.0 + mod_vector(1))[:, None] + mod_vector(0)[:, None]
    attended = spatial_attention(normed_t.astype(jnp.bfloat16), w_sqkv)
    attended = jnp.pad(
        attended.reshape(P_SIZE, -1, HALF), ((0, 0), (0, 0), (0, SLOT - HALF))
    ).reshape(P_SIZE, -1)
    slot_width = attended.shape[1]
    arrived = to_patches(jnp.concatenate([attended, latent], axis=1))
    attended = arrived[..., :slot_width].reshape(frames * pp, -1)
    residual = arrived[..., slot_width:].reshape(frames * pp, D).astype(jnp.float32)

    def rows_by(a, w):
        return jnp.einsum("rk,nk->rn", a, w, preferred_element_type=jnp.float32)

    stream = (residual + mod_vector(2) * bdot(attended, full_so)).astype(jnp.bfloat16)
    normed = branch_input(stream, mod_vector(3), mod_vector(4))
    q, k, v = (rows_by(normed, w).astype(jnp.bfloat16) for w in (wq, wk, wv))
    attended = temporal_attention(q, k, v, all_pos)
    stream = (stream.astype(jnp.float32) + mod_vector(5) * bdot(attended, full_to)).astype(
        jnp.bfloat16
    )
    normed = branch_input(stream, mod_vector(6), mod_vector(7))
    swap = [(i, i ^ 1) for i in range(frames)]
    both = jnp.concatenate([normed, lax.ppermute(normed, "frame", swap)], axis=0)
    half = mlp_blocks[0].shape[0] // 2
    first = jnp.concatenate([block[:half] for block in mlp_blocks], axis=0)
    second = jnp.concatenate([block[half:] for block in mlp_blocks], axis=0)
    hidden = jax.nn.gelu(rows_by(both, first), approximate=True).astype(jnp.bfloat16)
    total = bdot(hidden, second)
    count_rows = normed.shape[0]
    other = lax.ppermute(total[count_rows:].astype(jnp.bfloat16), "frame", swap)
    summed = total[:count_rows] + other.astype(jnp.float32)
    out = stream.astype(jnp.float32) + mod_vector(8) * summed
    return to_features(out.astype(jnp.bfloat16))


def solution(mesh):
    placed = (
        P("frame", "tensor"),
        P(),
        P("frame"),
        P(),
        P(None, "tensor"),
        P("tensor", None),
        P(None, "tensor"),
        P("tensor", None),
        P(None, "tensor"),
        P("tensor", None),
        P(None, "tensor"),
        P("tensor", None),
    )
    return jax.shard_map(
        shards, mesh=mesh, in_specs=placed, out_specs=P("frame", "tensor"), check_vma=False
    )
```
